128 devices in a mesh: side: 2 (over y_hi), tok: 4 (over x), vocab: 16 (over y_lo, z, core).
Axes of the slice: x: 4, y: 4 (y_hi: 2, y_lo: 2; y = y_hi * 2 + y_lo), z: 4, core: 2. Of those that a mesh axis runs over, the one named last changes fastest.
Arguments:
- teacher_hidden: bfloat16 [1024, 5120], P('tok', 'side'), may hold values from -48 to 48
- teacher_head: bfloat16 [5120, 38912], P('side', 'vocab'), may hold values from -1 to 1
- student_hidden: bfloat16 [1024, 4096], P('tok', 'side'), may hold values from -48 to 48
- student_head: bfloat16 [4096, 38912], P('side', 'vocab'), may hold values from -1 to 1
- sampled_ids: int32 [1024], P('tok'), may hold values from 0 to 38911
Outputs:
- token_kl: float32 [1024], P('tok')
- sampled_gap: float32 [1024], P('tok')
- hidden_grad: bfloat16 [1024, 4096], P('tok', ('side', 'vocab'))
- head_grad: float32 [4096, 38912], P(('side', 'tok'), 'vocab')
The draws below stay inside these ranges and needn't reach their ends.
All inputs are finite; a program needn't handle non-finite values.
Results may differ from the reference program's by a relative error of at most 0.009.
Values may be sent and summed in bfloat16 or wider, within the bound.
A program may use at most 128 MiB of HBM per device.

```python
import math
import jax
import jax.numpy as jnp

DT = 5120
DS = 4096
TOKENS = 1024
VOCAB = 38912


def head_table(key, row_count, col_count, salt):
    key = jax.random.fold_in(key, salt)
    values = jnp.clip(jax.random.normal(key, (row_count, col_count), jnp.float32), -5.0, 5.0)
    return values / math.sqrt(row_count)


def agreed_peaks(key):
    leader = jax.random.randint(jax.random.fold_in(key, 301), (TOKENS,), 0, VOCAB)
    strength = jax.random.uniform(jax.random.fold_in(key, 302), (TOKENS,), jnp.float32, 11.0, 13.0)
    return (leader, strength)


def unit_columns(table, picks):
    leading = table.T[picks]
    lead_norm = jnp.sum(leading * leading, axis=1, keepdims=True)
    return leading / lead_norm


def draw_teacher_head(key, part):
    table = head_table(key, DT, VOCAB, 101)
    return table.astype(jnp.bfloat16)


def draw_student_head(key, part):
    table = head_table(key, DS, VOCAB, 202)
    return table.astype(jnp.bfloat16)


def draw_teacher_hidden(key, part):
    leader, strength = agreed_peaks(key)
    table = head_table(key, DT, VOCAB, 101)
    values = jnp.clip(strength[:, None] * unit_columns(table, leader), -48.0, 48.0)
    return values.astype(jnp.bfloat16)


def draw_student_hidden(key, part):
    leader, strength = agreed_peaks(key)
    table = head_table(key, DS, VOCAB, 202)
    values = jnp.clip(strength[:, None] * unit_columns(table, leader), -48.0, 48.0)
    return values.astype(jnp.bfloat16)


def place_ends(array, key, least, top_value):
    longest = array.shape.index(max(array.shape))
    spots = []
    for shift in (0, 1):
        where = [jax.random.randint(jax.random.fold_in(key, axis), (), 0, length) for axis, length in enumerate(array.shape)]
        where[longest] = (where[longest] + shift) % array.shape[longest]
        spots.append(tuple(where))
    return array.at[spots[0]].set(least).at[spots[1]].set(top_value)


def setup_inputs(seed: int = 0) -> dict:
    splits = jax.random.split(jax.random.key(seed), 6)
    return {
        "teacher_hidden": draw_teacher_hidden(jax.random.fold_in(splits[5], 71), 0),
        "teacher_head": draw_teacher_head(jax.random.fold_in(splits[5], 71), 0),
        "student_hidden": draw_student_hidden(jax.random.fold_in(splits[5], 71), 0),
        "student_head": draw_student_head(jax.random.fold_in(splits[5], 71), 0),
        "sampled_ids": place_ends(jax.random.randint(splits[4], (TOKENS,), 0, VOCAB), jax.random.fold_in(splits[4], 1), 0, VOCAB - 1).astype(jnp.int32),
    }


def reference(teacher_hidden, teacher_head, student_hidden, student_head, sampled_ids):
    teacher_logits = jnp.dot(teacher_hidden, teacher_head, preferred_element_type=jnp.float32)
    student_logits = jnp.dot(student_hidden, student_head, preferred_element_type=jnp.float32)
    teacher_logp = teacher_logits - jax.nn.logsumexp(teacher_logits, axis=1)[:, None]
    student_logp = student_logits - jax.nn.logsumexp(student_logits, axis=1)[:, None]
    probs = jnp.exp(student_logp)
    token_kl = jnp.sum(probs * (student_logp - teacher_logp), axis=1)
    difference = student_logp - teacher_logp
    sampled_gap = jnp.take_along_axis(difference, sampled_ids[:, None].astype(jnp.int32), axis=1)[:, 0]
    logit_grad = (probs * (difference - token_kl[:, None])).astype(jnp.bfloat16)
    hidden_grad = jnp.dot(logit_grad, student_head.T, preferred_element_type=jnp.float32).astype(jnp.bfloat16)
    token_count = student_hidden.shape[0]
    head_grad = jnp.dot(student_hidden.T, logit_grad, preferred_element_type=jnp.float32) / token_count
    return (token_kl, sampled_gap, hidden_grad, head_grad.astype(jnp.float32))
```

```python
import functools

import jax
import jax.numpy as jnp
from jax import lax
from jax.experimental import pallas as pl
from jax.experimental.pallas import tpu as pltpu
from jax.sharding import PartitionSpec as P

MESH = pl.DeviceIdType.MESH
F32, BF16 = jnp.float32, jnp.bfloat16
CHUNKS = 4
LANES = 128
GROUP = 8
MIB = 1024 * 1024


def tiles(width, step):
    return [(at, min(step, width - at)) for at in range(0, width, step)]


def fold(parts):
    peak_s = functools.reduce(jnp.maximum, [p[0:1] for p in parts])
    peak_t = functools.reduce(jnp.maximum, [p[3:4] for p in parts])
    sum_s = weighted = sum_t = picked = jnp.zeros_like(peak_s)
    for p in parts:
        scale = jnp.exp(p[0:1] - peak_s)
        sum_s += p[1:2] * scale
        weighted += p[2:3] * scale
        sum_t += p[4:5] * jnp.exp(p[3:4] - peak_t)
        picked += p[5:6]
    return peak_s, sum_s, weighted, peak_t, sum_t, picked


def stack(rows):
    sub = lax.broadcasted_iota(jnp.int32, (8, LANES), 0)
    out = jnp.zeros((8, LANES), F32)
    for k, row in enumerate(rows):
        out = jnp.where(sub == k, row, out)
    return out


def main_kernel(
    th, sh, ids, thead, shead,
    g_out, ht_out, hid_out, kl_out, gap_out,
    wt, ws, pt, ps, rt, rs, gbuf, hall, ht,
    st_own, st_core, st_mid, st_grp, hg, hc, h2s, h2r, res, res_in,
    ls_sem, lt_sem, p_send, p_recv, cs_send, cs_recv, gs_send, gs_recv,
    y_send, y_recv, x_send, x_recv, l_sem, hx_send, hx_recv, hl_sem,
    hc_send, hc_recv, h2_send, h2_recv, r_send, r_recv,
):
    side, tok, voc = lax.axis_index("side"), lax.axis_index("tok"), lax.axis_index("vocab")
    core, grp = lax.rem(voc, 2), voc // 2
    side_peer = (1 - side, tok, voc)
    core_peer = (side, tok, voc + 1 - 2 * core)

    def x_at(k):
        return lax.rem(tok + k, 4)

    def x_peer(k):
        return (side, x_at(k), voc)

    def grp_at(k):
        return lax.rem(grp + k, GROUP)

    def grp_peer(k):
        return (side, tok, grp_at(k) * 2 + core)

    tokens, depth_s = sh.shape
    half = tokens // 2
    rows = half // CHUNKS
    width = ws.shape[1]
    feats = depth_s // 4
    blocks = width // LANES
    own0 = pl.multiple_of(side * half, half)
    far0 = pl.multiple_of((1 - side) * half, half)

    def remote(src, dst, send, recv, peer):
        return pltpu.make_async_remote_copy(
            src_ref=src, dst_ref=dst, send_sem=send, recv_sem=recv, device_id=peer, device_id_type=MESH
        )

    step = 256
    spans = tiles(width, step)

    def load(j, head, w, sem):
        at, n = spans[j]
        return pltpu.make_async_copy(head.at[:, pl.ds(at, n)], w.at[:, pl.ds(at, n)], sem.at[j])

    for j in range(len(spans)):
        load(j, shead, ws, ls_sem).start()
    for j in range(len(spans)):
        load(j, thead, wt, lt_sem).start()

    barrier = pltpu.get_barrier_semaphore()
    peers = [side_peer, core_peer] + [x_peer(k) for k in (1, 2, 3)] + [grp_peer(k) for k in range(1, GROUP)]
    for peer in peers:
        pl.semaphore_signal(barrier, inc=1, device_id=peer, device_id_type=MESH)
    pl.semaphore_wait(barrier, len(peers))

    def hidden_copy(k):
        return remote(
            sh.at[:, pl.ds(pl.multiple_of(x_at(k) * feats, feats), feats)],
            hall.at[tok],
            hx_send.at[k - 1],
            hx_recv.at[k - 1],
            x_peer(k),
        )

    for k in (1, 2, 3):
        hidden_copy(k).start()
    hidden_own = pltpu.make_async_copy(
        sh.at[:, pl.ds(pl.multiple_of(tok * feats, feats), feats)], hall.at[tok], hl_sem.at[0]
    )
    hidden_own.start()

    def matmul(h, head, w, sem, p):
        for j, (at, n) in enumerate(spans):
            load(j, head, w, sem).wait()
            p[:, at : at + n] = jnp.dot(h[...], w[:, at : at + n], preferred_element_type=F32)

    def partial_copy(model, c):
        src, dst = ((ps, rs), (pt, rt))[model]
        return remote(
            src.at[pl.ds(pl.multiple_of(far0 + c * rows, rows), rows), :],
            dst.at[pl.ds(c * rows, rows), :],
            p_send.at[model, c],
            p_recv.at[model, c],
            side_peer,
        )

    matmul(sh, shead, ws, ls_sem, ps)
    partial_copy(0, 0).start()
    matmul(th, thead, wt, lt_sem, pt)
    partial_copy(1, 0).start()
    partial_copy(0, 1).start()
    partial_copy(1, 1).start()

    hidden_own.wait()
    for k in (1, 2, 3):
        hidden_copy(k).wait()
    for k in range(4):
        ht[:, k * tokens : (k + 1) * tokens] = hall[k].T
    ht_copy = pltpu.make_async_copy(ht, ht_out, hl_sem.at[1])
    ht_copy.start()

    lane = lax.broadcasted_iota(jnp.int32, (rows, LANES), 1)
    sub = lax.broadcasted_iota(jnp.int32, (rows, LANES), 0)
    lane_row = lax.broadcasted_iota(jnp.int32, (1, LANES), 1)
    id_row = jnp.where(side == 0, ids[0:1, :], ids[1:2, :]).astype(F32)
    first = voc * width

    def core_stats(c):
        return remote(st_own.at[c], st_core.at[c], cs_send.at[c], cs_recv.at[c], core_peer)

    def grp_stats(c, k):
        return remote(st_mid.at[c], st_grp.at[c, grp], gs_send.at[c, k - 1], gs_recv.at[c, k - 1], grp_peer(k))

    def side_grad(c):
        return remote(gbuf.at[c, 0], gbuf.at[c, 1], y_send.at[c], y_recv.at[c], side_peer)

    def grad_rows(c, which):
        begin = tok * tokens + (own0 if which == 0 else far0) + c * rows
        return g_out.at[pl.ds(pl.multiple_of(begin, rows), rows), :]

    def x_grad(c, which, k):
        return remote(
            gbuf.at[c, which], grad_rows(c, which), x_send.at[c, which, k - 1], x_recv.at[c, which, k - 1], x_peer(k)
        )

    def local_grad(c, which):
        return pltpu.make_async_copy(gbuf.at[c, which], grad_rows(c, which), l_sem.at[c, which])

    def hidden_core(c):
        return remote(hg.at[c, 1 - core], hc.at[c], hc_send.at[c], hc_recv.at[c], core_peer)

    def hidden_grp(c, k):
        return remote(
            h2s.at[c, grp_at(k)], h2r.at[c, grp], h2_send.at[c, k - 1], h2_recv.at[c, k - 1], grp_peer(k)
        )

    def hidden_matmul(c, begin, end):
        g = gbuf[c].reshape(2 * rows, width)

        @pl.loop(begin, end)
        def _(f):
            w = ws[pl.ds(pl.multiple_of(f * 2 * LANES, 2 * LANES), 2 * LANES), :]
            r = lax.dot_general(g, w, (((1,), (1,)), ((), ())), preferred_element_type=F32).astype(BF16)
            hg[c, 0, f] = r[:, :LANES]
            hg[c, 1, f] = r[:, LANES:]

    def hidden_second(c):
        hidden_core(c).wait()
        h2s[c] = (hg[c, core].astype(F32) + hc[c].astype(F32)).astype(BF16)
        for k in range(1, GROUP):
            hidden_grp(c, k).start()

    def hidden_final(c):
        for k in range(1, GROUP):
            hidden_grp(c, k).wait()
        total = h2s[c, grp].astype(F32)
        for k in range(1, GROUP):
            total += h2r[c, grp_at(k)].astype(F32)
        total = total.astype(BF16)
        hid_out[pl.ds(pl.multiple_of(own0 + c * rows, rows), rows), :] = total[:rows]
        hid_out[pl.ds(pl.multiple_of(far0 + c * rows, rows), rows), :] = total[rows:]

    for c in range(CHUNKS):
        mine = pl.ds(pl.multiple_of(own0 + c * rows, rows), rows)
        theirs = pl.ds(c * rows, rows)
        eye = lane == sub + c * rows

        def to_row(col):
            return jnp.sum(jnp.where(eye, col, 0.0), axis=0, keepdims=True)

        def to_col(row):
            return jnp.sum(jnp.where(eye, row, 0.0), axis=1, keepdims=True)

        partial_copy(0, c).wait()
        partial_copy(1, c).wait()
        if c + 2 < CHUNKS:
            partial_copy(0, c + 2).start()
            partial_copy(1, c + 2).start()

        top_s = top_t = jnp.full((rows, LANES), -jnp.inf, F32)
        for j in range(blocks):
            cols = slice(j * LANES, (j + 1) * LANES)
            s = ps[mine, cols] + rs[theirs, cols]
            t = pt[mine, cols] + rt[theirs, cols]
            ps[mine, cols] = s
            pt[mine, cols] = t
            top_s, top_t = jnp.maximum(top_s, s), jnp.maximum(top_t, t)
        top_s = jnp.max(top_s, axis=1, keepdims=True)
        top_t = jnp.max(top_t, axis=1, keepdims=True)
        target = to_col(id_row).astype(jnp.int32) - first
        sum_s = weighted = sum_t = picked = jnp.zeros((rows, LANES), F32)
        for j in range(blocks):
            cols = slice(j * LANES, (j + 1) * LANES)
            s, t = ps[mine, cols], pt[mine, cols]
            e, d = jnp.exp(s - top_s), s - t
            sum_s += e
            weighted += e * d
            sum_t += jnp.exp(t - top_t)
            picked += jnp.where(lane + j * LANES == target, d, 0.0)
        sums = [jnp.sum(a, axis=1, keepdims=True) for a in (sum_s, weighted, sum_t, picked)]
        st_own[c] = stack([to_row(a) for a in (top_s, sums[0], sums[1], top_t, sums[2], sums[3])])
        core_stats(c).start()

        if c > 0:
            hidden_matmul(c - 1, 0, 2)

        core_stats(c).wait()
        st_mid[c] = stack(fold([st_own[c], st_core[c]]))
        for k in range(1, GROUP):
            grp_stats(c, k).start()

        if c > 0:
            hidden_matmul(c - 1, 2, 4)

        for k in range(1, GROUP):
            grp_stats(c, k).wait()
        parts = [st_mid[c]] + [st_grp[c, grp_at(k)] for k in range(1, GROUP)]
        peak_s, sum_s, weighted, peak_t, sum_t, picked = fold(parts)
        norm_s = peak_s + jnp.log(sum_s)
        norm_t = peak_t + jnp.log(sum_t)
        mean = weighted / sum_s
        here = (lane_row >= c * rows) & (lane_row < (c + 1) * rows)
        kl = jnp.where(here, mean - norm_s + norm_t, 0.0 if c == 0 else res[0:1])
        gap = jnp.where(here, picked - norm_s + norm_t, 0.0 if c == 0 else res[1:2])
        res[...] = stack([kl, gap])
        norm_col, mean_col = to_col(norm_s), to_col(mean)
        for j in range(blocks):
            cols = slice(j * LANES, (j + 1) * LANES)
            s, t = ps[mine, cols], pt[mine, cols]
            gbuf[c, 0, :, cols] = (jnp.exp(s - norm_col) * (s - t - mean_col)).astype(BF16)
        side_grad(c).start()
        for k in (1, 3, 2):
            x_grad(c, 0, k).start()
        local_grad(c, 0).start()

        if c > 0:
            hidden_matmul(c - 1, 4, GROUP)
            hidden_core(c - 1).start()

        side_grad(c).wait()
        for k in (1, 3, 2):
            x_grad(c, 1, k).start()
        local_grad(c, 1).start()
        if c > 0:
            hidden_second(c - 1)

    last = CHUNKS - 1
    row_copy = remote(res, res_in, r_send.at[0], r_recv.at[0], side_peer)
    row_copy.start()
    hidden_matmul(last, 0, GROUP)
    hidden_core(last).start()
    hidden_second(last)
    row_copy.wait()
    kl_out[0:1] = jnp.where(side == 0, res[0:1], res_in[0:1])
    kl_out[1:2] = jnp.where(side == 0, res_in[0:1], res[0:1])
    gap_out[0:1] = jnp.where(side == 0, res[1:2], res_in[1:2])
    gap_out[1:2] = jnp.where(side == 0, res_in[1:2], res[1:2])
    for c in range(CHUNKS):
        hidden_final(c)
    ht_copy.wait()
    for c in range(CHUNKS):
        for which in (0, 1):
            local_grad(c, which).wait()
            for k in (1, 2, 3):
                x_grad(c, which, k).wait()


def last_kernel(scale, ht, g, hid, kl, gap, out, hid_out, kl_out, gap_out):
    out[...] = jnp.dot(ht[...], g[...], preferred_element_type=F32) * scale

    @pl.when(pl.program_id(0) == 0)
    def _():
        hid_out[...] = hid[...]
        kl_out[...] = kl[...]
        gap_out[...] = gap[...]


def body(teacher_hidden, teacher_head, student_hidden, student_head, sampled_ids):
    tokens, depth_s = student_hidden.shape
    depth_t, width = teacher_head.shape
    toks = lax.axis_size("tok")
    half = tokens // 2
    rows = half // CHUNKS
    feats = depth_s // toks
    loads = len(tiles(width, 256))
    vmem, anywhere = pl.BlockSpec(memory_space=pltpu.VMEM), pl.BlockSpec(memory_space=pl.ANY)
    dma = pltpu.SemaphoreType.DMA
    g, ht, hid, kl, gap = pl.pallas_call(
        main_kernel,
        name="exchange",
        out_shape=(
            jax.ShapeDtypeStruct((toks * tokens, width), BF16),
            jax.ShapeDtypeStruct((feats, toks * tokens), BF16),
            jax.ShapeDtypeStruct((tokens, LANES), BF16),
            jax.ShapeDtypeStruct((2, LANES), F32),
            jax.ShapeDtypeStruct((2, LANES), F32),
        ),
        in_specs=[vmem, vmem, vmem, anywhere, anywhere],
        out_specs=(anywhere, anywhere, vmem, vmem, vmem),
        scratch_shapes=[
            pltpu.VMEM((depth_t, width), BF16),
            pltpu.VMEM((depth_s, width), BF16),
            pltpu.VMEM((tokens, width), F32),
            pltpu.VMEM((tokens, width), F32),
            pltpu.VMEM((half, width), F32),
            pltpu.VMEM((half, width), F32),
            pltpu.VMEM((CHUNKS, 2, rows, width), BF16),
            pltpu.VMEM((toks, tokens, feats), BF16),
            pltpu.VMEM((feats, toks * tokens), BF16),
            pltpu.VMEM((CHUNKS, 8, LANES), F32),
            pltpu.VMEM((CHUNKS, 8, LANES), F32),
            pltpu.VMEM((CHUNKS, 8, LANES), F32),
            pltpu.VMEM((CHUNKS, GROUP, 8, LANES), F32),
            pltpu.VMEM((CHUNKS, 2, GROUP, 2 * rows, LANES), BF16),
            pltpu.VMEM((CHUNKS, GROUP, 2 * rows, LANES), BF16),
            pltpu.VMEM((CHUNKS, GROUP, 2 * rows, LANES), BF16),
            pltpu.VMEM((CHUNKS, GROUP, 2 * rows, LANES), BF16),
            pltpu.VMEM((8, LANES), F32),
            pltpu.VMEM((8, LANES), F32),
            dma((loads,)),
            dma((loads,)),
            dma((2, CHUNKS)),
            dma((2, CHUNKS)),
            dma((CHUNKS,)),
            dma((CHUNKS,)),
            dma((CHUNKS, GROUP - 1)),
            dma((CHUNKS, GROUP - 1)),
            dma((CHUNKS,)),
            dma((CHUNKS,)),
            dma((CHUNKS, 2, 3)),
            dma((CHUNKS, 2, 3)),
            dma((CHUNKS, 2)),
            dma((3,)),
            dma((3,)),
            dma((2,)),
            dma((CHUNKS,)),
            dma((CHUNKS,)),
            dma((CHUNKS, GROUP - 1)),
            dma((CHUNKS, GROUP - 1)),
            dma((1,)),
            dma((1,)),
        ],
        compiler_params=pltpu.CompilerParams(
            collective_id=0, has_side_effects=True, vmem_limit_bytes=60 * MIB
        ),
    )(teacher_hidden, student_hidden, sampled_ids.reshape(2, LANES), teacher_head, student_head)

    step = 512
    whole = lambda a: pl.BlockSpec(a.shape, lambda j: (0,) * a.ndim)
    head_grad, hid, kl, gap = pl.pallas_call(
        functools.partial(last_kernel, 1.0 / (toks * tokens)),
        name="head_grad",
        grid=(pl.cdiv(width, step),),
        out_shape=(
            jax.ShapeDtypeStruct((feats, width), F32),
            jax.ShapeDtypeStruct(hid.shape, hid.dtype),
            jax.ShapeDtypeStruct(kl.shape, kl.dtype),
            jax.ShapeDtypeStruct(gap.shape, gap.dtype),
        ),
        in_specs=[whole(ht), pl.BlockSpec((toks * tokens, step), lambda j: (0, j)), whole(hid), whole(kl), whole(gap)],
        out_specs=(pl.BlockSpec((feats, step), lambda j: (0, j)), whole(hid), whole(kl), whole(gap)),
        compiler_params=pltpu.CompilerParams(vmem_limit_bytes=40 * MIB),
    )(ht, g, hid, kl, gap)
    return (kl.reshape(tokens), gap.reshape(tokens), hid, head_grad)


def solution(mesh):
    placed = (P("tok", "side"), P("side", "vocab"), P("tok", "side"), P("side", "vocab"), P("tok"))
    return jax.shard_map(
        body,
        mesh=mesh,
        in_specs=placed,
        out_specs=(P("tok"), P("tok"), P("tok", ("side", "vocab")), P(("side", "tok"), "vocab")),
        check_vma=False,
    )
```

```python
import functools

import jax
import jax.numpy as jnp
from jax import lax
from jax.experimental import pallas as pl
from jax.experimental.pallas import tpu as pltpu
from jax.sharding import PartitionSpec as P

MESH = pl.DeviceIdType.MESH
F32, BF16 = jnp.float32, jnp.bfloat16
CHUNKS = 8
PAIRS = CHUNKS // 2
LANES = 128
GROUP = 8
BITS = 21
TOP = float(2 ** (BITS - 1) - 1)
BIAS = 2 ** (BITS - 1)
MASK = 2**BITS - 1
LOW = 32 - BITS
LOAD = 512
MIB = 1024 * 1024
MAIN_VMEM, LAST_VMEM = 42, 16


def tiles(width, step):
    return [(at, min(step, width - at)) for at in range(0, width, step)]


def fold(parts):
    peak_s = functools.reduce(jnp.maximum, [p[0:1] for p in parts])
    peak_t = functools.reduce(jnp.maximum, [p[3:4] for p in parts])
    sum_s = weighted = sum_t = picked = jnp.zeros_like(peak_s)
    for p in parts:
        scale = jnp.exp(p[0:1] - peak_s)
        sum_s += p[1:2] * scale
        weighted += p[2:3] * scale
        sum_t += p[4:5] * jnp.exp(p[3:4] - peak_t)
        picked += p[5:6]
    return peak_s, sum_s, weighted, peak_t, sum_t, picked


def stack(rows):
    sub = lax.broadcasted_iota(jnp.int32, (8, LANES), 0)
    out = jnp.zeros((8, LANES), F32)
    for k, row in enumerate(rows):
        out = jnp.where(sub == k, row, out)
    return out


def encode(u, v, w):
    return u | (w << BITS), v | ((w >> LOW) << BITS)


def decode(a, b):
    high = lax.shift_right_logical(a, BITS) | (lax.shift_right_logical(b, BITS) << LOW)
    return a & MASK, b & MASK, high


def words(blocks):
    return 2 * (blocks // 3) + blocks % 3


def main_kernel(
    th_in, sh_in, ids, thead, shead,
    g_out, ht_out, hid_out, kl_out, gap_out,
    th, sh, wt, ws, pt, ps, wt_out, ws_out, wt_in, ws_in, gbuf, hall, ht,
    sc_out, sc_in, st_own, st_core, st_mid, st_grp, hg, hc, h2s, h2r, res, res_in,
    in_sem, ls_sem, lt_sem, sc_send, sc_recv, p_send, p_recv, cs_send, cs_recv, gs_send, gs_recv,
    y_send, y_recv, x_send, x_recv, l_sem, hx_send, hx_recv, hl_sem,
    hc_send, hc_recv, h2_send, h2_recv, r_send, r_recv,
):
    side, tok, voc = lax.axis_index("side"), lax.axis_index("tok"), lax.axis_index("vocab")
    core, grp = lax.rem(voc, 2), voc // 2
    side_peer = (1 - side, tok, voc)
    core_peer = (side, tok, voc + 1 - 2 * core)

    def x_at(k):
        return lax.rem(tok + k, 4)

    def x_peer(k):
        return (side, x_at(k), voc)

    def grp_at(k):
        return lax.rem(grp + k, GROUP)

    def grp_peer(k):
        return (side, tok, grp_at(k) * 2 + core)

    tokens, depth_s = sh.shape
    half = tokens // 2
    rows = half // CHUNKS
    pair_rows = 2 * rows
    width = ws.shape[1]
    feats = depth_s // 4
    blocks = width // LANES
    own0 = pl.multiple_of(side * half, half)
    far0 = pl.multiple_of((1 - side) * half, half)
    own, far = pl.ds(own0, half), pl.ds(far0, half)

    def remote(src, dst, send, recv, peer):
        return pltpu.make_async_remote_copy(
            src_ref=src, dst_ref=dst, send_sem=send, recv_sem=recv, device_id=peer, device_id_type=MESH
        )

    spans = tiles(width, LOAD)

    def load(j, head, w, sem):
        at, n = spans[j]
        return pltpu.make_async_copy(head.at[:, pl.ds(at, n)], w.at[:, pl.ds(at, n)], sem.at[j])

    sh_copy = pltpu.make_async_copy(sh_in, sh, in_sem.at[0])
    th_copy = pltpu.make_async_copy(th_in, th, in_sem.at[1])
    sh_copy.start()
    for j in range(len(spans)):
        load(j, shead, ws, ls_sem).start()
    th_copy.start()
    for j in range(len(spans)):
        load(j, thead, wt, lt_sem).start()

    barrier = pltpu.get_barrier_semaphore()
    peers = [side_peer, core_peer] + [x_peer(k) for k in (1, 2, 3)] + [grp_peer(k) for k in range(1, GROUP)]
    for peer in peers:
        pl.semaphore_signal(barrier, inc=1, device_id=peer, device_id_type=MESH)
    pl.semaphore_wait(barrier, len(peers))

    def hidden_copy(k):
        return remote(
            sh.at[:, pl.ds(pl.multiple_of(x_at(k) * feats, feats), feats)],
            hall.at[tok],
            hx_send.at[k - 1],
            hx_recv.at[k - 1],
            x_peer(k),
        )

    hidden_own = pltpu.make_async_copy(
        sh.at[:, pl.ds(pl.multiple_of(tok * feats, feats), feats)], hall.at[tok], hl_sem.at[0]
    )
    ht_copy = pltpu.make_async_copy(ht, ht_out, hl_sem.at[1])
    sh_copy.wait()
    for k in (1, 2, 3):
        hidden_copy(k).start()
    hidden_own.start()

    def transpose_hidden():
        hidden_own.wait()
        for k in (1, 2, 3):
            hidden_copy(k).wait()
        for k in range(4):
            ht[:, k * tokens : (k + 1) * tokens] = hall[k].T
        ht_copy.start()

    def matmul(h, head, w, sem, p):
        for j, (at, n) in enumerate(spans):
            load(j, head, w, sem).wait()
            p[:, at : at + n] = jnp.dot(h[...], w[:, at : at + n], preferred_element_type=F32)

    def scale_copy(model):
        return remote(sc_out.at[model], sc_in.at[model], sc_send.at[model], sc_recv.at[model], side_peer)

    def partial_copy(model, c):
        src, dst = ((ws_out, ws_in), (wt_out, wt_in))[model]
        at = pl.ds(c * rows, rows)
        return remote(src.at[at, :], dst.at[at, :], p_send.at[model, c], p_recv.at[model, c], side_peer)

    def code(model):
        p, out = ((ps, ws_out), (pt, wt_out))[model]
        top = jnp.zeros((half, LANES), F32)
        for j in range(blocks):
            top = jnp.maximum(top, jnp.abs(p[far, j * LANES : (j + 1) * LANES]))
        top = jnp.maximum(jnp.max(top, axis=1, keepdims=True), 1e-30)
        eye = lax.broadcasted_iota(jnp.int32, (half, LANES), 0) == lax.broadcasted_iota(jnp.int32, (half, LANES), 1)
        sc_out[model] = stack([jnp.sum(jnp.where(eye, top * (1.0 / TOP), 0.0), axis=0, keepdims=True)])
        scale_copy(model).start()
        inverse = TOP / top

        def codes(j):
            return (p[far, j * LANES : (j + 1) * LANES] * inverse + (BIAS + 0.5)).astype(jnp.int32)

        for k in range(blocks // 3):
            a, b = encode(codes(3 * k), codes(3 * k + 1), codes(3 * k + 2))
            out[:, 2 * k * LANES : (2 * k + 1) * LANES] = a
            out[:, (2 * k + 1) * LANES : (2 * k + 2) * LANES] = b
        for k in range(blocks % 3):
            at = (blocks // 3 * 2 + k) * LANES
            out[:, at : at + LANES] = codes(blocks // 3 * 3 + k)

    matmul(sh, shead, ws, ls_sem, ps)
    code(0)
    partial_copy(0, 0).start()
    partial_copy(0, 1).start()
    th_copy.wait()
    matmul(th, thead, wt, lt_sem, pt)
    code(1)
    partial_copy(1, 0).start()
    partial_copy(1, 1).start()

    lane = lax.broadcasted_iota(jnp.int32, (rows, LANES), 1)
    sub = lax.broadcasted_iota(jnp.int32, (rows, LANES), 0)
    lane_row = lax.broadcasted_iota(jnp.int32, (1, LANES), 1)
    id_row = jnp.where(side == 0, ids[0:1, :], ids[1:2, :]).astype(F32)
    first = voc * width

    def to_row(col, c):
        return jnp.sum(jnp.where(lane == sub + c * rows, col, 0.0), axis=0, keepdims=True)

    def to_col(row, c):
        return jnp.sum(jnp.where(lane == sub + c * rows, row, 0.0), axis=1, keepdims=True)

    def core_stats(c):
        return remote(st_own.at[c], st_core.at[c], cs_send.at[c], cs_recv.at[c], core_peer)

    def grp_stats(c, k):
        return remote(st_mid.at[c], st_grp.at[c, grp], gs_send.at[c, k - 1], gs_recv.at[c, k - 1], grp_peer(k))

    def grad_part(c, which):
        return gbuf.at[c // 2, which, pl.ds(c % 2 * rows, rows), :]

    def grad_rows(c, which):
        begin = tok * tokens + (own0 if which == 0 else far0) + c * rows
        return g_out.at[pl.ds(pl.multiple_of(begin, rows), rows), :]

    def side_grad(c):
        return remote(grad_part(c, 0), grad_part(c, 1), y_send.at[c], y_recv.at[c], side_peer)

    def x_grad(c, which, k):
        return remote(
            grad_part(c, which),
            grad_rows(c, which),
            x_send.at[c, which, k - 1],
            x_recv.at[c, which, k - 1],
            x_peer(k),
        )

    def local_grad(c, which):
        return pltpu.make_async_copy(grad_part(c, which), grad_rows(c, which), l_sem.at[c, which])

    def hidden_core(p):
        return remote(hg.at[p, 1 - core], hc.at[p], hc_send.at[p], hc_recv.at[p], core_peer)

    def hidden_grp(p, k):
        return remote(
            h2s.at[p, grp_at(k)], h2r.at[p, grp], h2_send.at[p, k - 1], h2_recv.at[p, k - 1], grp_peer(k)
        )

    def hidden_matmul(p, begin, end):
        g = gbuf[p].reshape(2 * pair_rows, width)

        @pl.loop(begin, end)
        def _(f):
            w = ws[pl.ds(pl.multiple_of(f * 2 * LANES, 2 * LANES), 2 * LANES), :]
            r = lax.dot_general(g, w, (((1,), (1,)), ((), ())), preferred_element_type=F32).astype(BF16)
            hg[p, 0, f] = r[:, :LANES]
            hg[p, 1, f] = r[:, LANES:]

    def hidden_second(p):
        hidden_core(p).wait()
        h2s[p] = (hg[p, core].astype(F32) + hc[p].astype(F32)).astype(BF16)
        for k in range(1, GROUP):
            hidden_grp(p, k).start()

    def hidden_final(p):
        for k in range(1, GROUP):
            hidden_grp(p, k).wait()
        total = h2s[p, grp].astype(F32)
        for k in range(1, GROUP):
            total += h2r[p, grp_at(k)].astype(F32)
        total = total.astype(BF16)
        hid_out[pl.ds(pl.multiple_of(own0 + p * pair_rows, pair_rows), pair_rows), :] = total[:pair_rows]
        hid_out[pl.ds(pl.multiple_of(far0 + p * pair_rows, pair_rows), pair_rows), :] = total[pair_rows:]

    def mine(c):
        return pl.ds(pl.multiple_of(own0 + c * rows, rows), rows)

    def sums_and_stats(c):
        tops = []
        for model, (p, w) in enumerate(((ps, ws_in), (pt, wt_in))):
            if c == 0:
                scale_copy(model).wait()
            partial_copy(model, c).wait()
            scale = to_col(sc_in[model, 0:1, :], c)
            top = jnp.full((rows, LANES), -jnp.inf, F32)
            theirs = pl.ds(c * rows, rows)

            def word(k):
                return w[theirs, k * LANES : (k + 1) * LANES]

            for k in range(blocks // 3):
                for n, u in enumerate(decode(word(2 * k), word(2 * k + 1))):
                    cols = slice((3 * k + n) * LANES, (3 * k + n + 1) * LANES)
                    v = p[mine(c), cols] + (u - BIAS).astype(F32) * scale
                    p[mine(c), cols] = v
                    top = jnp.maximum(top, v)
            for k in range(blocks % 3):
                at = (blocks // 3 * 3 + k) * LANES
                v = p[mine(c), at : at + LANES] + (word(blocks // 3 * 2 + k) - BIAS).astype(F32) * scale
                p[mine(c), at : at + LANES] = v
                top = jnp.maximum(top, v)
            tops.append(jnp.max(top, axis=1, keepdims=True))
        top_s, top_t = tops
        target = to_col(id_row, c).astype(jnp.int32) - first
        sum_s = weighted = sum_t = picked = jnp.zeros((rows, LANES), F32)
        for j in range(blocks):
            cols = slice(j * LANES, (j + 1) * LANES)
            s, t = ps[mine(c), cols], pt[mine(c), cols]
            e, d = jnp.exp(s - top_s), s - t
            sum_s += e
            weighted += e * d
            sum_t += jnp.exp(t - top_t)
            picked += jnp.where(lane + j * LANES == target, d, 0.0)
        sums = [jnp.sum(a, axis=1, keepdims=True) for a in (sum_s, weighted, sum_t, picked)]
        st_own[c] = stack([to_row(a, c) for a in (top_s, sums[0], sums[1], top_t, sums[2], sums[3])])
        core_stats(c).start()

    def join_core(c):
        core_stats(c).wait()
        st_mid[c] = stack(fold([st_own[c], st_core[c]]))
        for k in range(1, GROUP):
            grp_stats(c, k).start()

    def grads(c):
        for k in range(1, GROUP):
            grp_stats(c, k).wait()
        parts = [st_mid[c]] + [st_grp[c, grp_at(k)] for k in range(1, GROUP)]
        peak_s, sum_s, weighted, peak_t, sum_t, picked = fold(parts)
        norm_s = peak_s + jnp.log(sum_s)
        norm_t = peak_t + jnp.log(sum_t)
        mean = weighted / sum_s
        here = (lane_row >= c * rows) & (lane_row < (c + 1) * rows)
        kl = jnp.where(here, mean - norm_s + norm_t, 0.0 if c == 0 else res[0:1])
        gap = jnp.where(here, picked - norm_s + norm_t, 0.0 if c == 0 else res[1:2])
        res[...] = stack([kl, gap])
        norm_col, mean_col = to_col(norm_s, c), to_col(mean, c)
        for j in range(blocks):
            cols = slice(j * LANES, (j + 1) * LANES)
            s, t = ps[mine(c), cols], pt[mine(c), cols]
            v = (jnp.exp(s - norm_col) * (s - t - mean_col)).astype(BF16)
            gbuf[c // 2, 0, pl.ds(c % 2 * rows, rows), cols] = v
        side_grad(c).start()
        for k in (1, 3, 2):
            x_grad(c, 0, k).start()
        local_grad(c, 0).start()

    def forward(c):
        side_grad(c).wait()
        for k in (1, 3, 2):
            x_grad(c, 1, k).start()
        local_grad(c, 1).start()

    row_copy = remote(res, res_in, r_send.at[0], r_recv.at[0], side_peer)
    for i in range(CHUNKS + 2):
        if i < CHUNKS:
            sums_and_stats(i)
        if 1 <= i <= CHUNKS:
            grads(i - 1)
        if i == CHUNKS:
            row_copy.start()
        if i < CHUNKS:
            join_core(i)
        if i >= 2:
            forward(i - 2)
        if i + 2 < CHUNKS:
            partial_copy(0, i + 2).start()
            partial_copy(1, i + 2).start()
        if i == 1:
            transpose_hidden()
        if i >= 3 and i % 2 == 1:
            p = (i - 3) // 2
            if p > 0:
                hidden_second(p - 1)
            if i < CHUNKS + 1:
                hidden_matmul(p, 0, GROUP // 2)
        if i >= 4 and i % 2 == 0:
            p = (i - 4) // 2
            hidden_matmul(p, GROUP // 2, GROUP)
            hidden_core(p).start()

    last = PAIRS - 1
    hidden_matmul(last, 0, GROUP)
    hidden_core(last).start()
    row_copy.wait()
    kl_out[0:1] = jnp.where(side == 0, res[0:1], res_in[0:1])
    kl_out[1:2] = jnp.where(side == 0, res_in[0:1], res[0:1])
    gap_out[0:1] = jnp.where(side == 0, res[1:2], res_in[1:2])
    gap_out[1:2] = jnp.where(side == 0, res_in[1:2], res[1:2])
    for p in range(last):
        hidden_final(p)
    hidden_second(last)
    hidden_final(last)
    ht_copy.wait()
    for c in range(CHUNKS):
        for which in (0, 1):
            local_grad(c, which).wait()
            for k in (1, 2, 3):
                x_grad(c, which, k).wait()


def last_kernel(scale, ht, g, hid, kl, gap, out, hid_out, kl_out, gap_out):
    out[...] = jnp.dot(ht[...], g[...], preferred_element_type=F32) * scale

    @pl.when(pl.program_id(0) == 0)
    def _():
        hid_out[...] = hid[...]
        kl_out[...] = kl[...]
        gap_out[...] = gap[...]


def body(teacher_hidden, teacher_head, student_hidden, student_head, sampled_ids):
    tokens, depth_s = student_hidden.shape
    depth_t, width = teacher_head.shape
    toks = lax.axis_size("tok")
    half = tokens // 2
    feats = depth_s // toks
    pair_rows = half // PAIRS
    loads = len(tiles(width, LOAD))
    packed = words(width // LANES) * LANES
    vmem, anywhere = pl.BlockSpec(memory_space=pltpu.VMEM), pl.BlockSpec(memory_space=pl.ANY)
    dma = pltpu.SemaphoreType.DMA
    g, ht, hid, kl, gap = pl.pallas_call(
        main_kernel,
        name="exchange",
        out_shape=(
            jax.ShapeDtypeStruct((toks * tokens, width), BF16),
            jax.ShapeDtypeStruct((feats, toks * tokens), BF16),
            jax.ShapeDtypeStruct((tokens, LANES), BF16),
            jax.ShapeDtypeStruct((2, LANES), F32),
            jax.ShapeDtypeStruct((2, LANES), F32),
        ),
        in_specs=[anywhere, anywhere, vmem, anywhere, anywhere],
        out_specs=(anywhere, anywhere, vmem, vmem, vmem),
        scratch_shapes=[
            pltpu.VMEM((tokens, depth_t), BF16),
            pltpu.VMEM((tokens, depth_s), BF16),
            pltpu.VMEM((depth_t, width), BF16),
            pltpu.VMEM((depth_s, width), BF16),
            pltpu.VMEM((tokens, width), F32),
            pltpu.VMEM((tokens, width), F32),
            pltpu.VMEM((half, packed), jnp.int32),
            pltpu.VMEM((half, packed), jnp.int32),
            pltpu.VMEM((half, packed), jnp.int32),
            pltpu.VMEM((half, packed), jnp.int32),
            pltpu.VMEM((PAIRS, 2, pair_rows, width), BF16),
            pltpu.VMEM((toks, tokens, feats), BF16),
            pltpu.VMEM((feats, toks * tokens), BF16),
            pltpu.VMEM((2, 8, LANES), F32),
            pltpu.VMEM((2, 8, LANES), F32),
            pltpu.VMEM((CHUNKS, 8, LANES), F32),
            pltpu.VMEM((CHUNKS, 8, LANES), F32),
            pltpu.VMEM((CHUNKS, 8, LANES), F32),
            pltpu.VMEM((CHUNKS, GROUP, 8, LANES), F32),
            pltpu.VMEM((PAIRS, 2, GROUP, 2 * pair_rows, LANES), BF16),
            pltpu.VMEM((PAIRS, GROUP, 2 * pair_rows, LANES), BF16),
            pltpu.VMEM((PAIRS, GROUP, 2 * pair_rows, LANES), BF16),
            pltpu.VMEM((PAIRS, GROUP, 2 * pair_rows, LANES), BF16),
            pltpu.VMEM((8, LANES), F32),
            pltpu.VMEM((8, LANES), F32),
            dma((2,)),
            dma((loads,)),
            dma((loads,)),
            dma((2,)),
            dma((2,)),
            dma((2, CHUNKS)),
            dma((2, CHUNKS)),
            dma((CHUNKS,)),
            dma((CHUNKS,)),
            dma((CHUNKS, GROUP - 1)),
            dma((CHUNKS, GROUP - 1)),
            dma((CHUNKS,)),
            dma((CHUNKS,)),
            dma((CHUNKS, 2, 3)),
            dma((CHUNKS, 2, 3)),
            dma((CHUNKS, 2)),
            dma((3,)),
            dma((3,)),
            dma((2,)),
            dma((PAIRS,)),
            dma((PAIRS,)),
            dma((PAIRS, GROUP - 1)),
            dma((PAIRS, GROUP - 1)),
            dma((1,)),
            dma((1,)),
        ],
        compiler_params=pltpu.CompilerParams(
            collective_id=0, has_side_effects=True, vmem_limit_bytes=MAIN_VMEM * MIB
        ),
    )(teacher_hidden, student_hidden, sampled_ids.reshape(2, LANES), teacher_head, student_head)

    step = 512
    whole = lambda a: pl.BlockSpec(a.shape, lambda j: (0,) * a.ndim)
    head_grad, hid, kl, gap = pl.pallas_call(
        functools.partial(last_kernel, 1.0 / (toks * tokens)),
        name="head_grad",
        grid=(pl.cdiv(width, step),),
        out_shape=(
            jax.ShapeDtypeStruct((feats, width), F32),
            jax.ShapeDtypeStruct(hid.shape, hid.dtype),
            jax.ShapeDtypeStruct(kl.shape, kl.dtype),
            jax.ShapeDtypeStruct(gap.shape, gap.dtype),
        ),
        in_specs=[whole(ht), pl.BlockSpec((toks * tokens, step), lambda j: (0, j)), whole(hid), whole(kl), whole(gap)],
        out_specs=(pl.BlockSpec((feats, step), lambda j: (0, j)), whole(hid), whole(kl), whole(gap)),
        compiler_params=pltpu.CompilerParams(vmem_limit_bytes=LAST_VMEM * MIB),
    )(ht, g, hid, kl, gap)
    return (kl.reshape(tokens), gap.reshape(tokens), hid, head_grad)


def solution(mesh):
    placed = (P("tok", "side"), P("side", "vocab"), P("tok", "side"), P("side", "vocab"), P("tok"))
    return jax.shard_map(
        body,
        mesh=mesh,
        in_specs=placed,
        out_specs=(P("tok"), P("tok"), P("tok", ("side", "vocab")), P(("side", "tok"), "vocab")),
        check_vma=False,
    )
```

```python
import functools

import jax
import jax.numpy as jnp
from jax import lax
from jax.experimental import pallas as pl
from jax.experimental.pallas import tpu as pltpu
from jax.sharding import PartitionSpec as P

MESH = pl.DeviceIdType.MESH
F32, BF16 = jnp.float32, jnp.bfloat16
CHUNKS = 8
PAIRS = 2
PER = CHUNKS // PAIRS
AHEAD = 2
LANES = 128
GROUP = 8
BITS = 21
TOP = float(2 ** (BITS - 1) - 1)
BIAS = 2 ** (BITS - 1)
MASK = 2**BITS - 1
LOW = 32 - BITS
STEP = 512
MIB = 1024 * 1024
MAIN_VMEM, LAST_VMEM = 42, 16


def tiles(width, step):
    return [(at, min(step, width - at)) for at in range(0, width, step)]


def columns(width):
    blocks = width // LANES
    first = blocks // 6 * 3
    out = []
    for begin, end in ((0, first), (first, blocks)):
        middle = (begin + end + 1) // 2
        out += [(begin * LANES, (middle - begin) * LANES), (middle * LANES, (end - middle) * LANES)]
    return out


def fold(parts):
    peak_s = functools.reduce(jnp.maximum, [p[0:1] for p in parts])
    peak_t = functools.reduce(jnp.maximum, [p[3:4] for p in parts])
    sum_s = weighted = sum_t = picked = jnp.zeros_like(peak_s)
    for p in parts:
        scale = jnp.exp(p[0:1] - peak_s)
        sum_s += p[1:2] * scale
        weighted += p[2:3] * scale
        sum_t += p[4:5] * jnp.exp(p[3:4] - peak_t)
        picked += p[5:6]
    return peak_s, sum_s, weighted, peak_t, sum_t, picked


def stack(rows):
    sub = lax.broadcasted_iota(jnp.int32, (8, LANES), 0)
    out = jnp.zeros((8, LANES), F32)
    for k, row in enumerate(rows):
        out = jnp.where(sub == k, row, out)
    return out


def encode(u, v, w):
    return u | (w << BITS), v | ((w >> LOW) << BITS)


def decode(a, b):
    high = lax.shift_right_logical(a, BITS) | (lax.shift_right_logical(b, BITS) << LOW)
    return a & MASK, b & MASK, high


def words(blocks):
    return 2 * (blocks // 3) + blocks % 3


def main_kernel(
    th_in, sh_in, ids_in, thead, shead,
    g_out, ht_out, hid_out, kl_out, gap_out,
    ids, th, sh, wt, ws, pt, ps, wt_out, ws_out, wt_in, ws_in, gbuf, hall, ht,
    sc_out, sc_in, st_own, st_core, st_mid, st_grp, hg, hc, h2s, h2r, res, res_in,
    in_sem, ls_sem, lt_sem, sc_send, sc_recv, p_send, p_recv, cs_send, cs_recv, gs_send, gs_recv,
    y_send, y_recv, x_send, x_recv, l_sem, hx_send, hx_recv, hl_sem,
    hc_send, hc_recv, h2_send, h2_recv, r_send, r_recv,
):
    side, tok, voc = lax.axis_index("side"), lax.axis_index("tok"), lax.axis_index("vocab")
    core, grp = lax.rem(voc, 2), voc // 2
    side_peer = (1 - side, tok, voc)
    core_peer = (side, tok, voc + 1 - 2 * core)

    def x_at(k):
        return lax.rem(tok + k, 4)

    def x_peer(k):
        return (side, x_at(k), voc)

    def grp_at(k):
        return lax.rem(grp + k, GROUP)

    def grp_peer(k):
        return (side, tok, grp_at(k) * 2 + core)

    tokens, depth_s = sh.shape
    half = tokens // 2
    rows = half // CHUNKS
    pair_rows = PER * rows
    width = ws.shape[1]
    feats = depth_s // 4
    blocks = width // LANES
    own0 = pl.multiple_of(side * half, half)
    far0 = pl.multiple_of((1 - side) * half, half)
    own, far = pl.ds(own0, half), pl.ds(far0, half)

    def remote(src, dst, send, recv, peer):
        return pltpu.make_async_remote_copy(
            src_ref=src, dst_ref=dst, send_sem=send, recv_sem=recv, device_id=peer, device_id_type=MESH
        )

    spans = columns(width)

    def load(j, head, w, sem):
        at, n = spans[j]
        return pltpu.make_async_copy(head.at[:, pl.ds(at, n)], w.at[:, pl.ds(at, n)], sem.at[j])

    sh_copy = pltpu.make_async_copy(sh_in, sh, in_sem.at[0])
    th_copy = pltpu.make_async_copy(th_in, th, in_sem.at[1])
    sh_copy.start()
    for j in range(len(spans)):
        load(j, shead, ws, ls_sem).start()
    th_copy.start()
    for j in range(len(spans)):
        load(j, thead, wt, lt_sem).start()
    ids_copy = pltpu.make_async_copy(ids_in, ids, in_sem.at[2])
    ids_copy.start()

    barrier = pltpu.get_barrier_semaphore()
    peers = [side_peer, core_peer] + [x_peer(k) for k in (1, 2, 3)] + [grp_peer(k) for k in range(1, GROUP)]
    for peer in peers:
        pl.semaphore_signal(barrier, inc=1, device_id=peer, device_id_type=MESH)

    def hidden_copy(k):
        return remote(
            sh.at[:, pl.ds(pl.multiple_of(x_at(k) * feats, feats), feats)],
            hall.at[tok],
            hx_send.at[k - 1],
            hx_recv.at[k - 1],
            x_peer(k),
        )

    hidden_own = pltpu.make_async_copy(
        sh.at[:, pl.ds(pl.multiple_of(tok * feats, feats), feats)], hall.at[tok], hl_sem.at[0]
    )
    ht_copy = pltpu.make_async_copy(ht, ht_out, hl_sem.at[1])
    def transpose_hidden():
        hidden_own.wait()
        for k in (1, 2, 3):
            hidden_copy(k).wait()
        for k in range(4):
            ht[:, k * tokens : (k + 1) * tokens] = hall[k].T
        ht_copy.start()

    def matmul(h, head, w, sem, p, part):
        middle = len(spans) // 2
        for j in range(middle) if part == 0 else range(middle, len(spans)):
            at, n = spans[j]
            load(j, head, w, sem).wait()
            p[:, at : at + n] = jnp.dot(h[...], w[:, at : at + n], preferred_element_type=F32)

    def scale_copy(k):
        return remote(sc_out.at[k], sc_in.at[k], sc_send.at[k], sc_recv.at[k], side_peer)

    split = spans[len(spans) // 2][0] // LANES
    parts = ((0, split, 0, words(split)), (split, blocks - split, words(split), words(blocks - split)))

    def partial_copy(model, c):
        src, dst = ((ws_out, ws_in), (wt_out, wt_in))[model]
        at = pl.ds(c * rows, rows)
        return remote(src.at[at, :], dst.at[at, :], p_send.at[model, c], p_recv.at[model, c], side_peer)

    def early_copy(model, c, part):
        src, dst = ((ws_out, ws_in), (wt_out, wt_in))[model]
        at = pl.ds(c * rows, rows), pl.ds(parts[part][2] * LANES, parts[part][3] * LANES)
        n = part * CHUNKS + c
        return remote(src.at[at], dst.at[at], p_send.at[model, n], p_recv.at[model, n], side_peer)

    def code(model, part):
        p, out = ((ps, ws_out), (pt, wt_out))[model]
        block0, count, word0, _ = parts[part]
        top = jnp.zeros((half, LANES), F32)
        for j in range(block0, block0 + count):
            top = jnp.maximum(top, jnp.abs(p[far, j * LANES : (j + 1) * LANES]))
        top = jnp.maximum(jnp.max(top, axis=1, keepdims=True), 1e-30)
        eye = lax.broadcasted_iota(jnp.int32, (half, LANES), 0) == lax.broadcasted_iota(jnp.int32, (half, LANES), 1)
        sc_out[2 * model + part] = stack(
            [jnp.sum(jnp.where(eye, top * (1.0 / TOP), 0.0), axis=0, keepdims=True)]
        )
        scale_copy(2 * model + part).start()
        inverse = TOP / top

        def codes(j):
            at = (block0 + j) * LANES
            return (p[far, at : at + LANES] * inverse + (BIAS + 0.5)).astype(jnp.int32)

        def put(k, word):
            at = (word0 + k) * LANES
            out[:, at : at + LANES] = word

        for k in range(count // 3):
            a, b = encode(codes(3 * k), codes(3 * k + 1), codes(3 * k + 2))
            put(2 * k, a)
            put(2 * k + 1, b)
        for k in range(count % 3):
            put(count // 3 * 2 + k, codes(count // 3 * 3 + k))
        for c in range(AHEAD):
            early_copy(model, c, part).start()

    sh_copy.wait()
    matmul(sh, shead, ws, ls_sem, ps, 0)
    pl.semaphore_wait(barrier, len(peers))
    code(0, 0)
    matmul(sh, shead, ws, ls_sem, ps, 1)
    code(0, 1)
    for k in (1, 3, 2):
        hidden_copy(k).start()
    hidden_own.start()
    th_copy.wait()
    matmul(th, thead, wt, lt_sem, pt, 0)
    code(1, 0)
    matmul(th, thead, wt, lt_sem, pt, 1)
    code(1, 1)
    partial_copy(0, AHEAD).start()
    ids_copy.wait()

    lane = lax.broadcasted_iota(jnp.int32, (rows, LANES), 1)
    sub = lax.broadcasted_iota(jnp.int32, (rows, LANES), 0)
    lane_row = lax.broadcasted_iota(jnp.int32, (1, LANES), 1)
    id_row = jnp.where(side == 0, ids[0:1, :], ids[1:2, :]).astype(F32)
    first = voc * width

    def to_row(col, c):
        return jnp.sum(jnp.where(lane == sub + c * rows, col, 0.0), axis=0, keepdims=True)

    def to_col(row, c):
        return jnp.sum(jnp.where(lane == sub + c * rows, row, 0.0), axis=1, keepdims=True)

    def core_stats(c):
        return remote(st_own.at[c], st_core.at[c], cs_send.at[c], cs_recv.at[c], core_peer)

    def grp_stats(c, k):
        return remote(st_mid.at[c], st_grp.at[c, grp], gs_send.at[c, k - 1], gs_recv.at[c, k - 1], grp_peer(k))

    def grad_part(c, which):
        return gbuf.at[c // PER, which, pl.ds(c % PER * rows, rows), :]

    def grad_rows(c, which):
        begin = tok * tokens + (own0 if which == 0 else far0) + c * rows
        return g_out.at[pl.ds(pl.multiple_of(begin, rows), rows), :]

    def side_grad(c):
        return remote(grad_part(c, 0), grad_part(c, 1), y_send.at[c], y_recv.at[c], side_peer)

    def x_grad(c, which, k):
        return remote(
            grad_part(c, which),
            grad_rows(c, which),
            x_send.at[c, which, k - 1],
            x_recv.at[c, which, k - 1],
            x_peer(k),
        )

    def spread(c, which):
        for k in (1, 3, 2):
            x_grad(c, which, k).start()
        local_grad(c, which).start()

    def spread_end(c, which):
        local_grad(c, which).wait()
        for k in (1, 2, 3):
            x_grad(c, which, k).wait()

    def local_grad(c, which):
        return pltpu.make_async_copy(grad_part(c, which), grad_rows(c, which), l_sem.at[c, which])

    order = (*range(1, GROUP), 0)

    def hidden_core(p, k):
        f = grp_at(k)
        return remote(hg.at[p, 1 - core, f], hc.at[p, f], hc_send.at[p, k], hc_recv.at[p, k], core_peer)

    def hidden_grp(p, k):
        return remote(
            h2s.at[p, grp_at(k)], h2r.at[p, grp], h2_send.at[p, k - 1], h2_recv.at[p, k - 1], grp_peer(k)
        )

    def hidden_first(p, k):
        f = grp_at(k)
        w = ws[pl.ds(pl.multiple_of(f * 2 * LANES, 2 * LANES), 2 * LANES), :]
        g = gbuf[p].reshape(2 * pair_rows, width)
        r = lax.dot_general(g, w, (((1,), (1,)), ((), ())), preferred_element_type=F32).astype(BF16)
        hg[p, 0, f] = r[:, :LANES]
        hg[p, 1, f] = r[:, LANES:]
        hidden_core(p, k).start()

    def hidden_second(p, k):
        f = grp_at(k)
        hidden_core(p, k).wait()
        h2s[p, f] = (hg[p, core, f].astype(F32) + hc[p, f].astype(F32)).astype(BF16)
        if k > 0:
            hidden_grp(p, k).start()

    def hidden_steps(p, begin, end):
        for n in range(begin, end):
            if n < GROUP:
                hidden_first(p, order[n])
            if 0 <= n - 2 < GROUP:
                hidden_second(p, order[n - 2])

    def hidden_final(p):
        total = h2s[p, grp].astype(F32)
        for k in range(1, GROUP):
            hidden_grp(p, k).wait()
            total += h2r[p, grp_at(GROUP - k)].astype(F32)
        total = total.astype(BF16)
        hid_out[pl.ds(pl.multiple_of(own0 + p * pair_rows, pair_rows), pair_rows), :] = total[:pair_rows]
        hid_out[pl.ds(pl.multiple_of(far0 + p * pair_rows, pair_rows), pair_rows), :] = total[pair_rows:]

    def mine(c):
        return pl.ds(pl.multiple_of(own0 + c * rows, rows), rows)

    def sums_and_stats(c):
        tops = []
        for model, (p, w) in enumerate(((ps, ws_in), (pt, wt_in))):
            if c == 0:
                scale_copy(2 * model).wait()
                scale_copy(2 * model + 1).wait()
            if c < AHEAD:
                early_copy(model, c, 0).wait()
                early_copy(model, c, 1).wait()
            else:
                partial_copy(model, c).wait()
            top = jnp.full((rows, LANES), -jnp.inf, F32)
            theirs = pl.ds(c * rows, rows)
            for part, (block0, count, word0, _) in enumerate(parts):
                scale = to_col(sc_in[2 * model + part, 0:1, :], c)

                def word(k):
                    return w[theirs, (word0 + k) * LANES : (word0 + k + 1) * LANES]

                codes = [u for k in range(count // 3) for u in decode(word(2 * k), word(2 * k + 1))]
                codes += [word(count // 3 * 2 + k) for k in range(count % 3)]
                for k, u in enumerate(codes):
                    cols = slice((block0 + k) * LANES, (block0 + k + 1) * LANES)
                    v = p[mine(c), cols] + (u - BIAS).astype(F32) * scale
                    p[mine(c), cols] = v
                    top = jnp.maximum(top, v)
            tops.append(jnp.max(top, axis=1, keepdims=True))
        top_s, top_t = tops
        target = to_col(id_row, c).astype(jnp.int32) - first
        sum_s = weighted = sum_t = picked = jnp.zeros((rows, LANES), F32)
        for j in range(blocks):
            cols = slice(j * LANES, (j + 1) * LANES)
            s, t = ps[mine(c), cols], pt[mine(c), cols]
            e, d = jnp.exp(s - top_s), s - t
            sum_s += e
            weighted += e * d
            sum_t += jnp.exp(t - top_t)
            picked += jnp.where(lane + j * LANES == target, d, 0.0)
        sums = [jnp.sum(a, axis=1, keepdims=True) for a in (sum_s, weighted, sum_t, picked)]
        st_own[c] = stack([to_row(a, c) for a in (top_s, sums[0], sums[1], top_t, sums[2], sums[3])])
        core_stats(c).start()

    def join_core(c):
        core_stats(c).wait()
        st_mid[c] = stack(fold([st_own[c], st_core[c]]))
        for k in range(1, GROUP):
            grp_stats(c, k).start()

    def grads(c):
        for k in range(1, GROUP):
            grp_stats(c, k).wait()
        parts = [st_mid[c]] + [st_grp[c, grp_at(k)] for k in range(1, GROUP)]
        peak_s, sum_s, weighted, peak_t, sum_t, picked = fold(parts)
        norm_s = peak_s + jnp.log(sum_s)
        norm_t = peak_t + jnp.log(sum_t)
        mean = weighted / sum_s
        here = (lane_row >= c * rows) & (lane_row < (c + 1) * rows)
        kl = jnp.where(here, mean - norm_s + norm_t, 0.0 if c == 0 else res[0:1])
        gap = jnp.where(here, picked - norm_s + norm_t, 0.0 if c == 0 else res[1:2])
        res[...] = stack([kl, gap])
        norm_col, mean_col = to_col(norm_s, c), to_col(mean, c)
        for j in range(blocks):
            cols = slice(j * LANES, (j + 1) * LANES)
            s, t = ps[mine(c), cols], pt[mine(c), cols]
            v = (jnp.exp(s - norm_col) * (s - t - mean_col)).astype(BF16)
            gbuf[c // PER, 0, pl.ds(c % PER * rows, rows), cols] = v
        side_grad(c).start()
        spread(c, 0)

    def forward(c):
        side_grad(c).wait()
        spread(c, 1)

    row_copy = remote(res, res_in, r_send.at[0], r_recv.at[0], side_peer)
    for i in range(CHUNKS):
        end = i == CHUNKS - 1
        sums_and_stats(i)
        if end:
            join_core(i)
        if i >= 1:
            grads(i - 1)
        if not end:
            join_core(i)
        if AHEAD < i + 2 < CHUNKS:
            partial_copy(0, i + 2).start()
        if i + 2 < CHUNKS:
            partial_copy(1, i + 2).start()
        if i == 3:
            transpose_hidden()
        if i == PER + 1:
            hidden_steps(0, 0, GROUP // 2)
        if i == PER + 2:
            hidden_steps(0, GROUP // 2, GROUP + 2)
        if i >= 1 and not end:
            forward(i - 1)
    grads(CHUNKS - 1)
    row_copy.start()
    forward(CHUNKS - 2)
    hidden_final(0)
    forward(CHUNKS - 1)
    hidden_steps(1, 0, GROUP)
    row_copy.wait()
    kl_out[0:1] = jnp.where(side == 0, res[0:1], res_in[0:1])
    kl_out[1:2] = jnp.where(side == 0, res_in[0:1], res[0:1])
    gap_out[0:1] = jnp.where(side == 0, res[1:2], res_in[1:2])
    gap_out[1:2] = jnp.where(side == 0, res_in[1:2], res[1:2])
    hidden_steps(1, GROUP, GROUP + 2)
    hidden_final(1)
    ht_copy.wait()
    for c in range(CHUNKS):
        for which in (0, 1):
            spread_end(c, which)


def last_kernel(scale, ht, g, hid, kl, gap, out, hid_out, kl_out, gap_out, buf, sem):
    spans = tiles(g.shape[1], STEP)

    def store(j):
        at, n = spans[j]
        return pltpu.make_async_copy(buf.at[:, pl.ds(at, n)], out.at[:, pl.ds(at, n)], sem.at[j])

    for j, (at, n) in enumerate(spans):
        buf[:, at : at + n] = jnp.dot(ht[...], g[:, at : at + n], preferred_element_type=F32) * scale
        store(j).start()
    hid_out[...] = hid[...]
    kl_out[...] = kl[...]
    gap_out[...] = gap[...]
    for j in range(len(spans)):
        store(j).wait()


def body(teacher_hidden, teacher_head, student_hidden, student_head, sampled_ids):
    tokens, depth_s = student_hidden.shape
    depth_t, width = teacher_head.shape
    toks = lax.axis_size("tok")
    half = tokens // 2
    feats = depth_s // toks
    pair_rows = half // PAIRS
    loads = len(columns(width))
    middle = columns(width)[loads // 2][0] // LANES
    packed = (words(middle) + words(width // LANES - middle)) * LANES
    vmem, anywhere = pl.BlockSpec(memory_space=pltpu.VMEM), pl.BlockSpec(memory_space=pl.ANY)
    hbm = pl.BlockSpec(memory_space=pltpu.HBM)
    dma = pltpu.SemaphoreType.DMA
    g, ht, hid, kl, gap = pl.pallas_call(
        main_kernel,
        name="exchange",
        out_shape=(
            jax.ShapeDtypeStruct((toks * tokens, width), BF16),
            jax.ShapeDtypeStruct((feats, toks * tokens), BF16),
            jax.ShapeDtypeStruct((tokens, LANES), BF16),
            jax.ShapeDtypeStruct((2, LANES), F32),
            jax.ShapeDtypeStruct((2, LANES), F32),
        ),
        in_specs=[hbm] * 5,
        out_specs=(anywhere, anywhere, vmem, vmem, vmem),
        scratch_shapes=[
            pltpu.VMEM((2, LANES), jnp.int32),
            pltpu.VMEM((tokens, depth_t), BF16),
            pltpu.VMEM((tokens, depth_s), BF16),
            pltpu.VMEM((depth_t, width), BF16),
            pltpu.VMEM((depth_s, width), BF16),
            pltpu.VMEM((tokens, width), F32),
            pltpu.VMEM((tokens, width), F32),
            pltpu.VMEM((half, packed), jnp.int32),
            pltpu.VMEM((half, packed), jnp.int32),
            pltpu.VMEM((half, packed), jnp.int32),
            pltpu.VMEM((half, packed), jnp.int32),
            pltpu.VMEM((PAIRS, 2, pair_rows, width), BF16),
            pltpu.VMEM((toks, tokens, feats), BF16),
            pltpu.VMEM((feats, toks * tokens), BF16),
            pltpu.VMEM((4, 8, LANES), F32),
            pltpu.VMEM((4, 8, LANES), F32),
            pltpu.VMEM((CHUNKS, 8, LANES), F32),
            pltpu.VMEM((CHUNKS, 8, LANES), F32),
            pltpu.VMEM((CHUNKS, 8, LANES), F32),
            pltpu.VMEM((CHUNKS, GROUP, 8, LANES), F32),
            pltpu.VMEM((PAIRS, 2, GROUP, 2 * pair_rows, LANES), BF16),
            pltpu.VMEM((PAIRS, GROUP, 2 * pair_rows, LANES), BF16),
            pltpu.VMEM((PAIRS, GROUP, 2 * pair_rows, LANES), BF16),
            pltpu.VMEM((PAIRS, GROUP, 2 * pair_rows, LANES), BF16),
            pltpu.VMEM((8, LANES), F32),
            pltpu.VMEM((8, LANES), F32),
            dma((3,)),
            dma((loads,)),
            dma((loads,)),
            dma((4,)),
            dma((4,)),
            dma((2, CHUNKS + AHEAD)),
            dma((2, CHUNKS + AHEAD)),
            dma((CHUNKS,)),
            dma((CHUNKS,)),
            dma((CHUNKS, GROUP - 1)),
            dma((CHUNKS, GROUP - 1)),
            dma((CHUNKS,)),
            dma((CHUNKS,)),
            dma((CHUNKS, 2, 3)),
            dma((CHUNKS, 2, 3)),
            dma((CHUNKS, 2)),
            dma((3,)),
            dma((3,)),
            dma((2,)),
            dma((PAIRS, GROUP)),
            dma((PAIRS, GROUP)),
            dma((PAIRS, GROUP - 1)),
            dma((PAIRS, GROUP - 1)),
            dma((1,)),
            dma((1,)),
        ],
        compiler_params=pltpu.CompilerParams(
            collective_id=0, has_side_effects=True, vmem_limit_bytes=MAIN_VMEM * MIB
        ),
    )(
        *(
            pltpu.with_memory_space_constraint(a, pltpu.HBM)
            for a in (teacher_hidden, student_hidden, sampled_ids.reshape(2, LANES), teacher_head, student_head)
        )
    )

    head_grad, hid, kl, gap = pl.pallas_call(
        functools.partial(last_kernel, 1.0 / (toks * tokens)),
        name="head_grad",
        out_shape=(
            jax.ShapeDtypeStruct((feats, width), F32),
            jax.ShapeDtypeStruct(hid.shape, hid.dtype),
            jax.ShapeDtypeStruct(kl.shape, kl.dtype),
            jax.ShapeDtypeStruct(gap.shape, gap.dtype),
        ),
        in_specs=[vmem] * 5,
        out_specs=(anywhere, vmem, vmem, vmem),
        scratch_shapes=[pltpu.VMEM((feats, width), F32), dma((len(tiles(width, STEP)),))],
        compiler_params=pltpu.CompilerParams(vmem_limit_bytes=LAST_VMEM * MIB),
    )(ht, g, hid, kl, gap)
    return (kl.reshape(tokens), gap.reshape(tokens), hid, head_grad)


def solution(mesh):
    placed = (P("tok", "side"), P("side", "vocab"), P("tok", "side"), P("side", "vocab"), P("tok"))
    return jax.shard_map(
        body,
        mesh=mesh,
        in_specs=placed,
        out_specs=(P("tok"), P("tok"), P("tok", ("side", "vocab")), P(("side", "tok"), "vocab")),
        check_vma=False,
    )
```

```python
import functools

import jax
import jax.numpy as jnp
from jax import lax
from jax.experimental import pallas as pl
from jax.experimental.pallas import tpu as pltpu
from jax.sharding import PartitionSpec as P

MESH = pl.DeviceIdType.MESH
F32, BF16 = jnp.float32, jnp.bfloat16
CHUNKS = 8
PAIRS = 2
PER = CHUNKS // PAIRS
AHEAD = 2
LANES = 128
GROUP = 8
BITS = 21
TOP = float(2 ** (BITS - 1) - 1)
BIAS = 2 ** (BITS - 1)
MASK = 2**BITS - 1
LOW = 32 - BITS
STEP = 512
MIB = 1024 * 1024
MAIN_VMEM, LAST_VMEM = 42, 16


def tiles(width, step):
    return [(at, min(step, width - at)) for at in range(0, width, step)]


def columns(width):
    blocks = width // LANES
    first = blocks // 6 * 3
    out = []
    for begin, end in ((0, first), (first, blocks)):
        middle = (begin + end + 1) // 2
        out += [(begin * LANES, (middle - begin) * LANES), (middle * LANES, (end - middle) * LANES)]
    return out


def fold(parts):
    peak_s = functools.reduce(jnp.maximum, [p[0:1] for p in parts])
    peak_t = functools.reduce(jnp.maximum, [p[3:4] for p in parts])
    sum_s = weighted = sum_t = picked = jnp.zeros_like(peak_s)
    for p in parts:
        scale = jnp.exp(p[0:1] - peak_s)
        sum_s += p[1:2] * scale
        weighted += p[2:3] * scale
        sum_t += p[4:5] * jnp.exp(p[3:4] - peak_t)
        picked += p[5:6]
    return peak_s, sum_s, weighted, peak_t, sum_t, picked


def stack(rows):
    sub = lax.broadcasted_iota(jnp.int32, (8, LANES), 0)
    out = jnp.zeros((8, LANES), F32)
    for k, row in enumerate(rows):
        out = jnp.where(sub == k, row, out)
    return out


def encode(u, v, w):
    return u | (w << BITS), v | ((w >> LOW) << BITS)


def decode(a, b):
    high = lax.shift_right_logical(a, BITS) | (lax.shift_right_logical(b, BITS) << LOW)
    return a & MASK, b & MASK, high


def words(blocks):
    return 2 * (blocks // 3) + blocks % 3


def main_kernel(
    th_in, sh_in, ids_in, thead, shead,
    g_out, ht_out, hid_out, kl_out, gap_out,
    ids, th, sh, wt, ws, pt, ps, wt_out, ws_out, wt_in, ws_in, gbuf, hall, ht,
    sc_out, sc_in, st_own, st_core, st_mid, st_grp, hg, hc, h2s, h2r, res, res_in,
    in_sem, ls_sem, lt_sem, sc_send, sc_recv, p_send, p_recv, cs_send, cs_recv, gs_send, gs_recv,
    y_send, y_recv, x_send, x_recv, l_sem, hx_send, hx_recv, hl_sem,
    hc_send, hc_recv, h2_send, h2_recv, r_send, r_recv,
):
    side, tok, voc = lax.axis_index("side"), lax.axis_index("tok"), lax.axis_index("vocab")
    core, grp = lax.rem(voc, 2), voc // 2
    side_peer = (1 - side, tok, voc)
    core_peer = (side, tok, voc + 1 - 2 * core)

    def x_at(k):
        return lax.rem(tok + k, 4)

    def x_peer(k):
        return (side, x_at(k), voc)

    def grp_at(k):
        return lax.rem(grp + k, GROUP)

    def grp_peer(k):
        return (side, tok, grp_at(k) * 2 + core)

    tokens, depth_s = sh.shape
    half = tokens // 2
    rows = half // CHUNKS
    pair_rows = PER * rows
    width = ws.shape[1]
    feats = depth_s // 4
    blocks = width // LANES
    own0 = pl.multiple_of(side * half, half)
    far0 = pl.multiple_of((1 - side) * half, half)
    own, far = pl.ds(own0, half), pl.ds(far0, half)

    def remote(src, dst, send, recv, peer):
        return pltpu.make_async_remote_copy(
            src_ref=src, dst_ref=dst, send_sem=send, recv_sem=recv, device_id=peer, device_id_type=MESH
        )

    spans = columns(width)

    def load(j, head, w, sem):
        at, n = spans[j]
        return pltpu.make_async_copy(head.at[:, pl.ds(at, n)], w.at[:, pl.ds(at, n)], sem.at[j])

    sh_copy = pltpu.make_async_copy(sh_in, sh, in_sem.at[0])
    th_copy = pltpu.make_async_copy(th_in, th, in_sem.at[1])
    sh_copy.start()
    for j in range(len(spans)):
        load(j, shead, ws, ls_sem).start()
    th_copy.start()
    for j in range(len(spans)):
        load(j, thead, wt, lt_sem).start()
    ids_copy = pltpu.make_async_copy(ids_in, ids, in_sem.at[2])
    ids_copy.start()

    barrier = pltpu.get_barrier_semaphore()
    peers = [side_peer, core_peer] + [x_peer(k) for k in (1, 2, 3)] + [grp_peer(k) for k in range(1, GROUP)]
    for peer in peers:
        pl.semaphore_signal(barrier, inc=1, device_id=peer, device_id_type=MESH)

    def hidden_copy(k):
        return remote(
            sh.at[:, pl.ds(pl.multiple_of(x_at(k) * feats, feats), feats)],
            hall.at[tok],
            hx_send.at[k - 1],
            hx_recv.at[k - 1],
            x_peer(k),
        )

    hidden_own = pltpu.make_async_copy(
        sh.at[:, pl.ds(pl.multiple_of(tok * feats, feats), feats)], hall.at[tok], hl_sem.at[0]
    )
    ht_copy = pltpu.make_async_copy(ht, ht_out, hl_sem.at[1])
    def transpose_hidden():
        hidden_own.wait()
        for k in (1, 2, 3):
            hidden_copy(k).wait()
        for k in range(4):
            ht[:, k * tokens : (k + 1) * tokens] = hall[k].T
        ht_copy.start()

    def matmul(h, head, w, sem, p, part):
        middle = len(spans) // 2
        for j in range(middle) if part == 0 else range(middle, len(spans)):
            at, n = spans[j]
            load(j, head, w, sem).wait()
            p[:, at : at + n] = jnp.dot(h[...], w[:, at : at + n], preferred_element_type=F32)

    def scale_copy(k):
        return remote(sc_out.at[k], sc_in.at[k], sc_send.at[k], sc_recv.at[k], side_peer)

    split = spans[len(spans) // 2][0] // LANES
    parts = ((0, split, 0, words(split)), (split, blocks - split, words(split), words(blocks - split)))

    def partial_copy(model, c):
        src, dst = ((ws_out, ws_in), (wt_out, wt_in))[model]
        at = pl.ds(c * rows, rows)
        return remote(src.at[at, :], dst.at[at, :], p_send.at[model, c], p_recv.at[model, c], side_peer)

    def early_copy(model, c, part):
        src, dst = ((ws_out, ws_in), (wt_out, wt_in))[model]
        at = pl.ds(c * rows, rows), pl.ds(parts[part][2] * LANES, parts[part][3] * LANES)
        n = part * CHUNKS + c
        return remote(src.at[at], dst.at[at], p_send.at[model, n], p_recv.at[model, n], side_peer)

    def code(model, part):
        p, out = ((ps, ws_out), (pt, wt_out))[model]
        block0, count, word0, _ = parts[part]
        top = jnp.zeros((half, LANES), F32)
        for j in range(block0, block0 + count):
            top = jnp.maximum(top, jnp.abs(p[far, j * LANES : (j + 1) * LANES]))
        top = jnp.maximum(jnp.max(top, axis=1, keepdims=True), 1e-30)
        eye = lax.broadcasted_iota(jnp.int32, (half, LANES), 0) == lax.broadcasted_iota(jnp.int32, (half, LANES), 1)
        sc_out[2 * model + part] = stack(
            [jnp.sum(jnp.where(eye, top * (1.0 / TOP), 0.0), axis=0, keepdims=True)]
        )
        scale_copy(2 * model + part).start()
        inverse = TOP / top

        def codes(j):
            at = (block0 + j) * LANES
            return (p[far, at : at + LANES] * inverse + (BIAS + 0.5)).astype(jnp.int32)

        def put(k, word):
            at = (word0 + k) * LANES
            out[:, at : at + LANES] = word

        for k in range(count // 3):
            a, b = encode(codes(3 * k), codes(3 * k + 1), codes(3 * k + 2))
            put(2 * k, a)
            put(2 * k + 1, b)
        for k in range(count % 3):
            put(count // 3 * 2 + k, codes(count // 3 * 3 + k))
        for c in range(AHEAD):
            early_copy(model, c, part).start()

    sh_copy.wait()
    matmul(sh, shead, ws, ls_sem, ps, 0)
    pl.semaphore_wait(barrier, len(peers))
    code(0, 0)
    matmul(sh, shead, ws, ls_sem, ps, 1)
    code(0, 1)
    for k in (1, 3, 2):
        hidden_copy(k).start()
    hidden_own.start()
    th_copy.wait()
    matmul(th, thead, wt, lt_sem, pt, 0)
    code(1, 0)
    matmul(th, thead, wt, lt_sem, pt, 1)
    code(1, 1)
    partial_copy(0, AHEAD).start()
    ids_copy.wait()

    lane = lax.broadcasted_iota(jnp.int32, (rows, LANES), 1)
    sub = lax.broadcasted_iota(jnp.int32, (rows, LANES), 0)
    lane_row = lax.broadcasted_iota(jnp.int32, (1, LANES), 1)
    id_row = jnp.where(side == 0, ids[0:1, :], ids[1:2, :]).astype(F32)
    first = voc * width

    def to_row(col, c):
        return jnp.sum(jnp.where(lane == sub + c * rows, col, 0.0), axis=0, keepdims=True)

    def to_col(row, c):
        return jnp.sum(jnp.where(lane == sub + c * rows, row, 0.0), axis=1, keepdims=True)

    def core_stats(c):
        return remote(st_own.at[c], st_core.at[c], cs_send.at[c], cs_recv.at[c], core_peer)

    def grp_stats(c, k):
        return remote(st_mid.at[c], st_grp.at[c, grp], gs_send.at[c, k - 1], gs_recv.at[c, k - 1], grp_peer(k))

    def grad_part(c, which):
        return gbuf.at[c // PER, which, pl.ds(c % PER * rows, rows), :]

    def grad_rows(c, which):
        begin = tok * tokens + (own0 if which == 0 else far0) + c * rows
        return g_out.at[pl.ds(pl.multiple_of(begin, rows), rows), :]

    def side_grad(c):
        return remote(grad_part(c, 0), grad_part(c, 1), y_send.at[c], y_recv.at[c], side_peer)

    def x_grad(c, which, k):
        return remote(
            grad_part(c, which),
            grad_rows(c, which),
            x_send.at[c, which, k - 1],
            x_recv.at[c, which, k - 1],
            x_peer(k),
        )

    def spread(c, which):
        for k in (1, 3, 2):
            x_grad(c, which, k).start()
        local_grad(c, which).start()

    def spread_end(c, which):
        local_grad(c, which).wait()
        for k in (1, 2, 3):
            x_grad(c, which, k).wait()

    def local_grad(c, which):
        return pltpu.make_async_copy(grad_part(c, which), grad_rows(c, which), l_sem.at[c, which])

    order = (*range(1, GROUP), 0)

    def hidden_core(p, k):
        f = grp_at(k)
        return remote(hg.at[p, 1 - core, f], hc.at[p, f], hc_send.at[p, k], hc_recv.at[p, k], core_peer)

    def hidden_grp(p, k):
        return remote(
            h2s.at[p, grp_at(k)], h2r.at[p, grp], h2_send.at[p, k - 1], h2_recv.at[p, k - 1], grp_peer(k)
        )

    def hidden_first(p, k):
        f = grp_at(k)
        w = ws[pl.ds(pl.multiple_of(f * 2 * LANES, 2 * LANES), 2 * LANES), :]
        g = gbuf[p].reshape(2 * pair_rows, width)
        r = lax.dot_general(g, w, (((1,), (1,)), ((), ())), preferred_element_type=F32).astype(BF16)
        hg[p, 0, f] = r[:, :LANES]
        hg[p, 1, f] = r[:, LANES:]
        hidden_core(p, k).start()

    def hidden_second(p, k):
        f = grp_at(k)
        hidden_core(p, k).wait()
        h2s[p, f] = (hg[p, core, f].astype(F32) + hc[p, f].astype(F32)).astype(BF16)
        if k > 0:
            hidden_grp(p, k).start()

    def hidden_steps(p, begin, end):
        for n in range(begin, end):
            if n < GROUP:
                hidden_first(p, order[n])
            if 0 <= n - 2 < GROUP:
                hidden_second(p, order[n - 2])

    def hidden_final(p):
        total = h2s[p, grp].astype(F32)
        for k in range(1, GROUP):
            hidden_grp(p, k).wait()
            total += h2r[p, grp_at(GROUP - k)].astype(F32)
        total = total.astype(BF16)
        hid_out[pl.ds(pl.multiple_of(own0 + p * pair_rows, pair_rows), pair_rows), :] = total[:pair_rows]
        hid_out[pl.ds(pl.multiple_of(far0 + p * pair_rows, pair_rows), pair_rows), :] = total[pair_rows:]

    def mine(c):
        return pl.ds(pl.multiple_of(own0 + c * rows, rows), rows)

    def sums_and_stats(c):
        tops = []
        for model, (p, w) in enumerate(((ps, ws_in), (pt, wt_in))):
            if c == 0:
                scale_copy(2 * model).wait()
                scale_copy(2 * model + 1).wait()
            if c < AHEAD:
                early_copy(model, c, 0).wait()
                early_copy(model, c, 1).wait()
            else:
                partial_copy(model, c).wait()
            top = jnp.full((rows, LANES), -jnp.inf, F32)
            theirs = pl.ds(c * rows, rows)
            for part, (block0, count, word0, _) in enumerate(parts):
                scale = to_col(sc_in[2 * model + part, 0:1, :], c)

                def word(k):
                    return w[theirs, (word0 + k) * LANES : (word0 + k + 1) * LANES]

                codes = [u for k in range(count // 3) for u in decode(word(2 * k), word(2 * k + 1))]
                codes += [word(count // 3 * 2 + k) for k in range(count % 3)]
                for k, u in enumerate(codes):
                    cols = slice((block0 + k) * LANES, (block0 + k + 1) * LANES)
                    v = p[mine(c), cols] + (u - BIAS).astype(F32) * scale
                    p[mine(c), cols] = v
                    top = jnp.maximum(top, v)
            tops.append(jnp.max(top, axis=1, keepdims=True))
        top_s, top_t = tops
        target = to_col(id_row, c).astype(jnp.int32) - first
        sum_s = weighted = sum_t = picked = jnp.zeros((rows, LANES), F32)
        for j in range(blocks):
            cols = slice(j * LANES, (j + 1) * LANES)
            s, t = ps[mine(c), cols], pt[mine(c), cols]
            e, d = jnp.exp(s - top_s), s - t
            sum_s += e
            weighted += e * d
            sum_t += jnp.exp(t - top_t)
            picked += jnp.where(lane + j * LANES == target, d, 0.0)
        sums = [jnp.sum(a, axis=1, keepdims=True) for a in (sum_s, weighted, sum_t, picked)]
        st_own[c] = stack([to_row(a, c) for a in (top_s, sums[0], sums[1], top_t, sums[2], sums[3])])
        core_stats(c).start()

    def join_core(c):
        core_stats(c).wait()
        st_mid[c] = stack(fold([st_own[c], st_core[c]]))
        for k in range(1, GROUP):
            grp_stats(c, k).start()

    def grads(c):
        for k in range(1, GROUP):
            grp_stats(c, k).wait()
        parts = [st_mid[c]] + [st_grp[c, grp_at(k)] for k in range(1, GROUP)]
        peak_s, sum_s, weighted, peak_t, sum_t, picked = fold(parts)
        norm_s = peak_s + jnp.log(sum_s)
        norm_t = peak_t + jnp.log(sum_t)
        mean = weighted / sum_s
        here = (lane_row >= c * rows) & (lane_row < (c + 1) * rows)
        kl = jnp.where(here, mean - norm_s + norm_t, 0.0 if c == 0 else res[0:1])
        gap = jnp.where(here, picked - norm_s + norm_t, 0.0 if c == 0 else res[1:2])
        res[...] = stack([kl, gap])
        norm_col, mean_col = to_col(norm_s, c), to_col(mean, c)
        for j in range(blocks):
            cols = slice(j * LANES, (j + 1) * LANES)
            s, t = ps[mine(c), cols], pt[mine(c), cols]
            v = (jnp.exp(s - norm_col) * (s - t - mean_col)).astype(BF16)
            gbuf[c // PER, 0, pl.ds(c % PER * rows, rows), cols] = v
        side_grad(c).start()
        spread(c, 0)

    def forward(c):
        side_grad(c).wait()
        spread(c, 1)

    row_copy = remote(res, res_in, r_send.at[0], r_recv.at[0], side_peer)
    for i in range(CHUNKS):
        end = i == CHUNKS - 1
        sums_and_stats(i)
        join_core(i)
        if i >= 1:
            grads(i - 1)
        if AHEAD < i + 2 < CHUNKS:
            partial_copy(0, i + 2).start()
        if i + 2 < CHUNKS:
            partial_copy(1, i + 2).start()
        if i == 3:
            transpose_hidden()
        if i == PER + 1:
            hidden_steps(0, 0, GROUP // 2)
        if i == PER + 2:
            hidden_steps(0, GROUP // 2, GROUP + 2)
        if i >= 1 and not end:
            forward(i - 1)
    grads(CHUNKS - 1)
    row_copy.start()
    forward(CHUNKS - 2)
    hidden_final(0)
    forward(CHUNKS - 1)
    hidden_steps(1, 0, GROUP)
    row_copy.wait()
    kl_out[0:1] = jnp.where(side == 0, res[0:1], res_in[0:1])
    kl_out[1:2] = jnp.where(side == 0, res_in[0:1], res[0:1])
    gap_out[0:1] = jnp.where(side == 0, res[1:2], res_in[1:2])
    gap_out[1:2] = jnp.where(side == 0, res_in[1:2], res[1:2])
    hidden_steps(1, GROUP, GROUP + 2)
    hidden_final(1)
    ht_copy.wait()
    for c in range(CHUNKS):
        for which in (0, 1):
            spread_end(c, which)


def last_kernel(scale, ht, g, hid, kl, gap, out, hid_out, kl_out, gap_out, buf, sem):
    spans = tiles(g.shape[1], STEP)

    def store(j):
        at, n = spans[j]
        return pltpu.make_async_copy(buf.at[:, pl.ds(at, n)], out.at[:, pl.ds(at, n)], sem.at[j])

    for j, (at, n) in enumerate(spans):
        buf[:, at : at + n] = jnp.dot(ht[...], g[:, at : at + n], preferred_element_type=F32) * scale
        store(j).start()
    hid_out[...] = hid[...]
    kl_out[...] = kl[...]
    gap_out[...] = gap[...]
    for j in range(len(spans)):
        store(j).wait()


def body(teacher_hidden, teacher_head, student_hidden, student_head, sampled_ids):
    tokens, depth_s = student_hidden.shape
    depth_t, width = teacher_head.shape
    toks = lax.axis_size("tok")
    half = tokens // 2
    feats = depth_s // toks
    pair_rows = half // PAIRS
    loads = len(columns(width))
    middle = columns(width)[loads // 2][0] // LANES
    packed = (words(middle) + words(width // LANES - middle)) * LANES
    vmem, anywhere = pl.BlockSpec(memory_space=pltpu.VMEM), pl.BlockSpec(memory_space=pl.ANY)
    hbm = pl.BlockSpec(memory_space=pltpu.HBM)
    dma = pltpu.SemaphoreType.DMA
    g, ht, hid, kl, gap = pl.pallas_call(
        main_kernel,
        name="exchange",
        out_shape=(
            jax.ShapeDtypeStruct((toks * tokens, width), BF16),
            jax.ShapeDtypeStruct((feats, toks * tokens), BF16),
            jax.ShapeDtypeStruct((tokens, LANES), BF16),
            jax.ShapeDtypeStruct((2, LANES), F32),
            jax.ShapeDtypeStruct((2, LANES), F32),
        ),
        in_specs=[hbm] * 5,
        out_specs=(anywhere, anywhere, vmem, vmem, vmem),
        scratch_shapes=[
            pltpu.VMEM((2, LANES), jnp.int32),
            pltpu.VMEM((tokens, depth_t), BF16),
            pltpu.VMEM((tokens, depth_s), BF16),
            pltpu.VMEM((depth_t, width), BF16),
            pltpu.VMEM((depth_s, width), BF16),
            pltpu.VMEM((tokens, width), F32),
            pltpu.VMEM((tokens, width), F32),
            pltpu.VMEM((half, packed), jnp.int32),
            pltpu.VMEM((half, packed), jnp.int32),
            pltpu.VMEM((half, packed), jnp.int32),
            pltpu.VMEM((half, packed), jnp.int32),
            pltpu.VMEM((PAIRS, 2, pair_rows, width), BF16),
            pltpu.VMEM((toks, tokens, feats), BF16),
            pltpu.VMEM((feats, toks * tokens), BF16),
            pltpu.VMEM((4, 8, LANES), F32),
            pltpu.VMEM((4, 8, LANES), F32),
            pltpu.VMEM((CHUNKS, 8, LANES), F32),
            pltpu.VMEM((CHUNKS, 8, LANES), F32),
            pltpu.VMEM((CHUNKS, 8, LANES), F32),
            pltpu.VMEM((CHUNKS, GROUP, 8, LANES), F32),
            pltpu.VMEM((PAIRS, 2, GROUP, 2 * pair_rows, LANES), BF16),
            pltpu.VMEM((PAIRS, GROUP, 2 * pair_rows, LANES), BF16),
            pltpu.VMEM((PAIRS, GROUP, 2 * pair_rows, LANES), BF16),
            pltpu.VMEM((PAIRS, GROUP, 2 * pair_rows, LANES), BF16),
            pltpu.VMEM((8, LANES), F32),
            pltpu.VMEM((8, LANES), F32),
            dma((3,)),
            dma((loads,)),
            dma((loads,)),
            dma((4,)),
            dma((4,)),
            dma((2, CHUNKS + AHEAD)),
            dma((2, CHUNKS + AHEAD)),
            dma((CHUNKS,)),
            dma((CHUNKS,)),
            dma((CHUNKS, GROUP - 1)),
            dma((CHUNKS, GROUP - 1)),
            dma((CHUNKS,)),
            dma((CHUNKS,)),
            dma((CHUNKS, 2, 3)),
            dma((CHUNKS, 2, 3)),
            dma((CHUNKS, 2)),
            dma((3,)),
            dma((3,)),
            dma((2,)),
            dma((PAIRS, GROUP)),
            dma((PAIRS, GROUP)),
            dma((PAIRS, GROUP - 1)),
            dma((PAIRS, GROUP - 1)),
            dma((1,)),
            dma((1,)),
        ],
        compiler_params=pltpu.CompilerParams(
            collective_id=0, has_side_effects=True, vmem_limit_bytes=MAIN_VMEM * MIB
        ),
    )(
        *(
            pltpu.with_memory_space_constraint(a, pltpu.HBM)
            for a in (teacher_hidden, student_hidden, sampled_ids.reshape(2, LANES), teacher_head, student_head)
        )
    )

    head_grad, hid, kl, gap = pl.pallas_call(
        functools.partial(last_kernel, 1.0 / (toks * tokens)),
        name="head_grad",
        out_shape=(
            jax.ShapeDtypeStruct((feats, width), F32),
            jax.ShapeDtypeStruct(hid.shape, hid.dtype),
            jax.ShapeDtypeStruct(kl.shape, kl.dtype),
            jax.ShapeDtypeStruct(gap.shape, gap.dtype),
        ),
        in_specs=[vmem] * 5,
        out_specs=(anywhere, vmem, vmem, vmem),
        scratch_shapes=[pltpu.VMEM((feats, width), F32), dma((len(tiles(width, STEP)),))],
        compiler_params=pltpu.CompilerParams(vmem_limit_bytes=LAST_VMEM * MIB),
    )(ht, g, hid, kl, gap)
    return (kl.reshape(tokens), gap.reshape(tokens), hid, head_grad)


def solution(mesh):
    placed = (P("tok", "side"), P("side", "vocab"), P("tok", "side"), P("side", "vocab"), P("tok"))
    return jax.shard_map(
        body,
        mesh=mesh,
        in_specs=placed,
        out_specs=(P("tok"), P("tok"), P("tok", ("side", "vocab")), P(("side", "tok"), "vocab")),
        check_vma=False,
    )
```
